32 devices in a mesh: ctx: 8 (over y, x, core), head: 4 (over z).
Axes of the slice: x: 2, y: 2, z: 4, core: 2. Of those that a mesh axis runs over, the one named last changes fastest.
Arguments:
- hidden: bfloat16 [4096, 5376], P('ctx'), may hold values from -18 to 18
- w_query: bfloat16 [5376, 2048], P(None, 'head'), may hold values from -0.078125 to 0.078125
- key_weight_matrix: bfloat16 [5376, 1024], P(None, 'head'), may hold values from -0.078125 to 0.078125
- value_weight_matrix: bfloat16 [5376, 1024], P(None, 'head'), may hold values from -0.078125 to 0.078125
- attention_output_gradient: bfloat16 [4096, 2048], P('ctx', 'head'), may hold values from -6 to 6
- doc_start: int32 [4096], P('ctx'), may hold values from 0 to 4095, as said below
Outputs:
- d_hidden: float32 [4096, 5376], P(('ctx', 'head'))
The draws below stay inside these ranges and needn't reach their ends.
Inputs may be any that keep to these rules, and one draw needn't show every extreme that they name: doc_start is non-decreasing, doc_start[i] <= i, constant within a document and equal to i at a document's first token; doc_start[0] = 0, and the last token begins a document of its own.
All inputs are finite; a program needn't handle non-finite values.
Results may differ from the reference program's by a relative error of at most 0.014.
The reference program's roundings to bfloat16 on the way (of `probability_low`, `d_scores` and `d_query`) count: a program that leaves them out, or rounds other values in their place, can miss the bound.
Values may be sent and summed in bfloat16 or wider, within the bound.
No kernel may reach another device: no remote copies, remote signals or barrier semaphores. Data moves between devices by JAX's collectives and lax.ppermute only.
A program may use at most 128 MiB of HBM per device.

```python
import jax
import jax.numpy as jnp
from jax import lax

MODEL_WIDTH = 5376
QUERY_HEADS = 16
KEY_VALUE_HEADS = 8
HEAD_SIZE = 128
W = 1024
LOCAL_TOKENS = 512
SEQUENCE_TOKENS = 4096
HALO = 2


def draw_hidden(key, part):
    first_key = jax.random.fold_in(key, 11)
    entries = jnp.clip(jax.random.normal(first_key, (SEQUENCE_TOKENS, MODEL_WIDTH), jnp.float32), -4.0, 4.0)
    return entries.astype(jnp.bfloat16)


def draw_doc_start(key, part):
    marks = jax.random.randint(jax.random.fold_in(key, 21), (SEQUENCE_TOKENS,), 0, 4 * W)
    positions = jnp.arange(SEQUENCE_TOKENS, dtype=jnp.int32)
    opening = (marks == 0) | (positions == 0) | (positions == SEQUENCE_TOKENS - 1)
    starts = jnp.where(opening, positions, 0).astype(jnp.int32)
    return lax.cummax(starts, axis=0)


def level_of(own_key, extent, cuts, least, largest):
    level, own = 1.0, jax.random.fold_in(own_key, 6)
    for axis_at, shards_of in cuts:
        draws = jnp.exp(jax.random.uniform(jax.random.fold_in(own, axis_at), (shards_of,), jnp.float32, least / len(cuts), largest / len(cuts)))
        level = level * jnp.repeat(draws, extent[axis_at] // shards_of).reshape([-1 if axis == axis_at else 1 for axis in range(len(extent))])
    return level


def gaussian(own_key, dims, scale, reach, cuts=(), kind=jnp.bfloat16):
    level = level_of(own_key, dims, cuts, -0.22, 0.18) if cuts else 1.0
    values = jax.random.normal(own_key, dims, jnp.float32) * scale * level
    return jnp.minimum(jnp.maximum(values, -reach), reach).astype(kind)


def setup_inputs(seed: int = 0) -> dict:
    arg_keys = jax.random.split(jax.random.key(seed), 7)
    hidden = draw_hidden(jax.random.fold_in(arg_keys[6], 71), 0)
    w_query = gaussian(arg_keys[1], (MODEL_WIDTH, QUERY_HEADS * HEAD_SIZE), MODEL_WIDTH ** -0.5, 0.078125, ((1, 4),))
    key_weight_matrix = gaussian(arg_keys[2], (MODEL_WIDTH, KEY_VALUE_HEADS * HEAD_SIZE), MODEL_WIDTH ** -0.5, 0.078125, ((1, 4),))
    value_weight_matrix = gaussian(arg_keys[3], (MODEL_WIDTH, KEY_VALUE_HEADS * HEAD_SIZE), MODEL_WIDTH ** -0.5, 0.078125, ((1, 4),))
    attention_output_gradient = gaussian(arg_keys[4], (SEQUENCE_TOKENS, QUERY_HEADS * HEAD_SIZE), 1.0, 6.0, ((0, 8), (1, 4)))
    doc_start = draw_doc_start(jax.random.fold_in(arg_keys[6], 71), 0)
    return dict(hidden=hidden, w_query=w_query, key_weight_matrix=key_weight_matrix, value_weight_matrix=value_weight_matrix, attention_output_gradient=attention_output_gradient, doc_start=doc_start)


SCALE = 168.0 ** -0.5


def masked_scores(query_rows, key_tile_block, query_position, lower_bound, key_position):
    scores = jnp.einsum("ikgd,jkd->kgij", query_rows.astype(jnp.float32), key_tile_block.astype(jnp.float32)) * SCALE
    allowed = (key_position[None, :] >= lower_bound[:, None]) & (key_position[None, :] <= query_position[:, None])
    return jnp.where(allowed[None, None], scores, -jnp.inf)


def block_backward(query_rows, output_gradient, key_tile_block, value_tile_block, query_position, lower_bound, key_position):
    scores = masked_scores(query_rows, key_tile_block, query_position, lower_bound, key_position)
    row_max = jnp.max(scores, axis=-1, keepdims=True)
    denominator = jnp.sum(jnp.exp(scores - row_max), axis=-1, keepdims=True)
    probability = jnp.exp(scores - (row_max + jnp.log(denominator)))
    probability_low = probability.astype(jnp.bfloat16)
    output = jnp.einsum("kgij,jkd->ikgd", probability_low.astype(jnp.float32), value_tile_block.astype(jnp.float32))
    row_dot = jnp.einsum("ikgd,ikgd->kgi", output_gradient.astype(jnp.float32), output)
    d_probs = jnp.einsum("ikgd,jkd->kgij", output_gradient.astype(jnp.float32), value_tile_block.astype(jnp.float32))
    d_scores = (probability * (d_probs - row_dot[..., None]) * SCALE).astype(jnp.bfloat16)
    d_query = jnp.einsum("kgij,jkd->ikgd", d_scores.astype(jnp.float32), key_tile_block.astype(jnp.float32))
    d_key = jnp.einsum("kgij,ikgd->jkd", d_scores.astype(jnp.float32), query_rows.astype(jnp.float32))
    d_value = jnp.einsum("kgij,ikgd->jkd", probability_low.astype(jnp.float32), output_gradient.astype(jnp.float32))
    return d_query, d_key, d_value


def back_project(grad, weight):
    return lax.dot_general(grad, weight, (((1,), (1,)), ((), ())), preferred_element_type=jnp.float32)


def reference(hidden, w_query, key_weight_matrix, value_weight_matrix, attention_output_gradient, doc_start):
    query_group_count = QUERY_HEADS // KEY_VALUE_HEADS
    query_rows = jnp.dot(hidden, w_query, preferred_element_type=jnp.float32).astype(jnp.bfloat16)
    projected_keys = jnp.dot(hidden, key_weight_matrix, preferred_element_type=jnp.float32).astype(jnp.bfloat16)
    projected_values = jnp.dot(hidden, value_weight_matrix, preferred_element_type=jnp.float32).astype(jnp.bfloat16)
    padding_rows = HALO * LOCAL_TOKENS
    covered_rows = (HALO + 1) * LOCAL_TOKENS
    padded_keys = jnp.concatenate([jnp.zeros((padding_rows, KEY_VALUE_HEADS * HEAD_SIZE), jnp.bfloat16), projected_keys], axis=0)
    padded_values = jnp.concatenate([jnp.zeros((padding_rows, KEY_VALUE_HEADS * HEAD_SIZE), jnp.bfloat16), projected_values], axis=0)
    positions = jnp.arange(SEQUENCE_TOKENS, dtype=jnp.int32)
    lower_all = jnp.maximum(doc_start, positions - W + 1)

    def attend_block(running, block_index):
        d_key_all, d_value_all = running
        leading_row = (block_index * LOCAL_TOKENS).astype(jnp.int32)
        query_tile_block = lax.dynamic_slice_in_dim(query_rows, leading_row, LOCAL_TOKENS, 0).reshape(LOCAL_TOKENS, KEY_VALUE_HEADS, query_group_count, HEAD_SIZE)
        output_gradient = lax.dynamic_slice_in_dim(attention_output_gradient, leading_row, LOCAL_TOKENS, 0).reshape(LOCAL_TOKENS, KEY_VALUE_HEADS, query_group_count, HEAD_SIZE)
        key_tile_block = lax.dynamic_slice_in_dim(padded_keys, leading_row, covered_rows, 0).reshape(covered_rows, KEY_VALUE_HEADS, HEAD_SIZE)
        value_tile_block = lax.dynamic_slice_in_dim(padded_values, leading_row, covered_rows, 0).reshape(covered_rows, KEY_VALUE_HEADS, HEAD_SIZE)
        query_position = leading_row + jnp.arange(LOCAL_TOKENS, dtype=jnp.int32)
        lower_bound = lax.dynamic_slice_in_dim(lower_all, leading_row, LOCAL_TOKENS, 0)
        key_position = leading_row - padding_rows + jnp.arange(covered_rows, dtype=jnp.int32)
        d_query, d_key, d_value = block_backward(query_tile_block, output_gradient, key_tile_block, value_tile_block, query_position, lower_bound, key_position)
        d_key_all = lax.dynamic_update_slice_in_dim(d_key_all, lax.dynamic_slice_in_dim(d_key_all, leading_row, covered_rows, 0) + d_key, leading_row, 0)
        d_value_all = lax.dynamic_update_slice_in_dim(d_value_all, lax.dynamic_slice_in_dim(d_value_all, leading_row, covered_rows, 0) + d_value, leading_row, 0)
        return (d_key_all, d_value_all), d_query.reshape(LOCAL_TOKENS, QUERY_HEADS * HEAD_SIZE)

    initial_state = (jnp.zeros((SEQUENCE_TOKENS + padding_rows, KEY_VALUE_HEADS, HEAD_SIZE), jnp.float32), jnp.zeros((SEQUENCE_TOKENS + padding_rows, KEY_VALUE_HEADS, HEAD_SIZE), jnp.float32))
    closing_state, d_query_blocks = lax.scan(attend_block, initial_state, jnp.arange(SEQUENCE_TOKENS // LOCAL_TOKENS, dtype=jnp.int32))
    d_query = d_query_blocks.reshape(SEQUENCE_TOKENS, QUERY_HEADS * HEAD_SIZE).astype(jnp.bfloat16)
    key_gradient_rows = closing_state[0][padding_rows:].reshape(SEQUENCE_TOKENS, KEY_VALUE_HEADS * HEAD_SIZE).astype(jnp.bfloat16)
    value_gradient_rows = closing_state[1][padding_rows:].reshape(SEQUENCE_TOKENS, KEY_VALUE_HEADS * HEAD_SIZE).astype(jnp.bfloat16)
    summed = back_project(d_query, w_query)
    summed = summed + back_project(key_gradient_rows, key_weight_matrix)
    summed = summed + back_project(value_gradient_rows, value_weight_matrix)
    return summed
```

```python
import functools

import jax
import jax.numpy as jnp
from jax import lax
from jax.experimental import pallas as pl
from jax.experimental.pallas import tpu as pltpu
from jax.sharding import PartitionSpec as P

HEAD_SIZE = 128
W = 1024
HALO = 2
SCALE = 168.0 ** (-0.5)
LOG2E = 1.4426950408889634
BLOCK = 128
MASKED = -1e30
VMEM_LIMIT = 48 * 1024 * 1024

NT = (((1,), (1,)), ((), ()))


def project_kernel(hidden_ref, wk_ref, wv_ref, *refs):
    outs, acc_ref = refs[:-1], refs[-1]
    step = pl.program_id(0)
    width = wk_ref.shape[1]

    @pl.when(step == 0)
    def _():
        acc_ref[...] = jnp.zeros_like(acc_ref)

    hidden = hidden_ref[...]
    acc_ref[:, :width] += jnp.dot(hidden, wk_ref[...], preferred_element_type=jnp.float32)
    acc_ref[:, width:] += jnp.dot(hidden, wv_ref[...], preferred_element_type=jnp.float32)

    @pl.when(step == pl.num_programs(0) - 1)
    def _():
        for head, out in enumerate(outs):
            cols = slice(head * HEAD_SIZE, (head + 1) * HEAD_SIZE)
            out[:, :HEAD_SIZE] = acc_ref[:, cols].astype(out.dtype)
            cols = slice(width + head * HEAD_SIZE, width + (head + 1) * HEAD_SIZE)
            out[:, HEAD_SIZE:] = acc_ref[:, cols].astype(out.dtype)


def project_keys_values(hidden, wk, wv):
    rows, depth = hidden.shape
    width = wk.shape[1]
    heads = width // HEAD_SIZE
    tile = 896
    return pl.pallas_call(
        project_kernel,
        grid=(depth // tile,),
        in_specs=[
            pl.BlockSpec((rows, tile), lambda k: (0, k)),
            pl.BlockSpec((tile, width), lambda k: (k, 0)),
            pl.BlockSpec((tile, width), lambda k: (k, 0)),
        ],
        out_specs=[pl.BlockSpec((rows, 2 * HEAD_SIZE), lambda k: (0, 0))] * heads,
        out_shape=[jax.ShapeDtypeStruct((rows, 2 * HEAD_SIZE), jnp.bfloat16)] * heads,
        scratch_shapes=[pltpu.VMEM((rows, 2 * width), jnp.float32)],
        compiler_params=pltpu.CompilerParams(vmem_limit_bytes=VMEM_LIMIT),
        cost_estimate=pl.CostEstimate(
            flops=4 * rows * depth * width,
            bytes_accessed=2 * (rows * depth + 2 * depth * width),
            transcendentals=0,
        ),
        name="project_kv",
    )(hidden, wk, wv)


def attention_kernel(
    q_ref, do_ref, far_ref, near_ref, own_ref, low_ref,
    dq_ref, gfar_ref, gnear_ref, gown_ref,
    k_ref, v_ref, dkt_ref, dvt_ref,
):
    rows = q_ref.shape[0]
    window = W + BLOCK
    for at, ref in enumerate((far_ref, near_ref, own_ref)):
        k_ref[at * rows : (at + 1) * rows, :] = ref[:, :HEAD_SIZE]
        v_ref[at * rows : (at + 1) * rows, :] = ref[:, HEAD_SIZE:]
    dkt_ref[...] = jnp.zeros_like(dkt_ref)
    dvt_ref[...] = jnp.zeros_like(dvt_ref)
    for block in range(rows // BLOCK):
        at = slice(block * BLOCK, (block + 1) * BLOCK)
        span = slice(block * BLOCK, block * BLOCK + window)
        q = jnp.concatenate([q_ref[at, :HEAD_SIZE], q_ref[at, HEAD_SIZE:]], axis=0)
        do = jnp.concatenate([do_ref[at, :HEAD_SIZE], do_ref[at, HEAD_SIZE:]], axis=0)
        k = k_ref[span, :]
        v = v_ref[span, :]
        low = low_ref[at, :]
        low = jnp.concatenate([low, low], axis=0) - block * BLOCK
        scores = lax.dot_general(q, k, NT, preferred_element_type=jnp.float32)
        col = lax.broadcasted_iota(jnp.int32, scores.shape, 1)
        row = lax.broadcasted_iota(jnp.int32, scores.shape, 0) & (BLOCK - 1)
        allowed = (col >= low) & (col <= row + W)
        scores = jnp.where(allowed, scores * (SCALE * LOG2E), MASKED)
        top = jnp.max(scores, axis=1, keepdims=True)
        e = jnp.exp2(scores - top)
        inverse = 1.0 / jnp.sum(e, axis=1, keepdims=True)
        probability = e * inverse
        probability_low = probability.astype(jnp.bfloat16)
        d_probs = lax.dot_general(do, v, NT, preferred_element_type=jnp.float32)
        row_dot = jnp.sum(
            probability_low.astype(jnp.float32) * d_probs, axis=1, keepdims=True
        )
        d_scores = (probability * ((d_probs - row_dot) * SCALE)).astype(jnp.bfloat16)
        dq = jnp.dot(d_scores, k, preferred_element_type=jnp.float32).astype(dq_ref.dtype)
        dq_ref[at, :HEAD_SIZE] = dq[:BLOCK]
        dq_ref[at, HEAD_SIZE:] = dq[BLOCK:]
        dkt_ref[:, span] += jnp.dot(q.T, d_scores, preferred_element_type=jnp.float32)
        dvt_ref[:, span] += jnp.dot(do.T, probability_low, preferred_element_type=jnp.float32)
    for at, ref in enumerate((gfar_ref, gnear_ref, gown_ref)):
        part = slice(at * rows, (at + 1) * rows)
        ref[:, :HEAD_SIZE] = dkt_ref[:, part].T.astype(ref.dtype)
        ref[:, HEAD_SIZE:] = dvt_ref[:, part].T.astype(ref.dtype)


def attend(head, queries, cotangent, far, near, own, low):
    rows = queries.shape[0]
    pair = 2 * HEAD_SIZE
    covered = (HALO + 1) * rows
    whole = pl.BlockSpec((rows, pair), lambda i: (0, 0))
    column = pl.BlockSpec((rows, pair), lambda i: (0, head))
    work = 2 * rows * (W + BLOCK) * HEAD_SIZE
    return pl.pallas_call(
        attention_kernel,
        grid=(1,),
        in_specs=[column, column, whole, whole, whole, pl.BlockSpec((rows, 1), lambda i: (0, 0))],
        out_specs=[whole] * 4,
        out_shape=[
            jax.ShapeDtypeStruct((rows, pair), jnp.bfloat16),
            jax.ShapeDtypeStruct((rows, pair), jnp.bfloat16),
            jax.ShapeDtypeStruct((rows, pair), jnp.bfloat16),
            jax.ShapeDtypeStruct((rows, pair), jnp.float32),
        ],
        scratch_shapes=[
            pltpu.VMEM((covered, HEAD_SIZE), jnp.bfloat16),
            pltpu.VMEM((covered, HEAD_SIZE), jnp.bfloat16),
            pltpu.VMEM((HEAD_SIZE, covered), jnp.float32),
            pltpu.VMEM((HEAD_SIZE, covered), jnp.float32),
        ],
        compiler_params=pltpu.CompilerParams(vmem_limit_bytes=VMEM_LIMIT),
        cost_estimate=pl.CostEstimate(
            flops=16 * work, bytes_accessed=16 * rows * pair, transcendentals=work // HEAD_SIZE
        ),
        name="attention",
    )(queries, cotangent, far, near, own, low)


def back_kernel(dq0_ref, dq1_ref, g0_ref, g1_ref, wq_ref, wk_ref, wv_ref, out_ref):
    def nt(x, w):
        return lax.dot_general(x, w, NT, preferred_element_type=jnp.float32)

    pair = 2 * HEAD_SIZE
    total = nt(dq0_ref[...], wq_ref[:, :pair]) + nt(dq1_ref[...], wq_ref[:, pair:])
    dk = jnp.concatenate([g0_ref[:, :HEAD_SIZE], g1_ref[:, :HEAD_SIZE]], axis=1)
    dv = jnp.concatenate([g0_ref[:, HEAD_SIZE:], g1_ref[:, HEAD_SIZE:]], axis=1)
    out_ref[...] = (total + nt(dk, wk_ref[...]) + nt(dv, wv_ref[...])).astype(out_ref.dtype)


def back_project(dq0, dq1, g0, g1, wq, wk, wv, part, parts):
    rows = dq0.shape[0]
    pair = 2 * HEAD_SIZE
    columns = wq.shape[0] // parts
    tile = columns // 2
    first = part * 2
    whole = pl.BlockSpec((rows, pair), lambda j: (0, 0))
    return pl.pallas_call(
        back_kernel,
        grid=(columns // tile,),
        in_specs=[whole] * 4
        + [pl.BlockSpec((tile, w.shape[1]), lambda j: (first + j, 0)) for w in (wq, wk, wv)],
        out_specs=pl.BlockSpec((rows, tile), lambda j: (0, j)),
        out_shape=jax.ShapeDtypeStruct((rows, columns), jnp.bfloat16),
        compiler_params=pltpu.CompilerParams(vmem_limit_bytes=VMEM_LIMIT),
        cost_estimate=pl.CostEstimate(
            flops=8 * rows * columns * pair,
            bytes_accessed=2 * columns * (4 * pair + rows),
            transcendentals=0,
        ),
        name="back_project",
    )(dq0, dq1, g0, g1, wq, wk, wv)


def shards(hidden, w_query, w_key, w_value, cotangent, doc_start):
    rows = hidden.shape[0]
    contexts = lax.axis_size("ctx")
    planes = lax.axis_size("head")
    ctx = lax.axis_index("ctx")
    plane = lax.axis_index("head")
    odd = (ctx % 2) == 1
    heads = w_key.shape[1] // HEAD_SIZE
    swap = [(i, i ^ 1) for i in range(contexts)]
    ahead = [(i, i + 2) for i in range(contexts - 2)]
    behind = [(i + 2, i) for i in range(contexts - 2)]

    low = jnp.maximum(
        doc_start - ctx * rows + HALO * rows,
        jnp.arange(rows, dtype=jnp.int32) + (HALO * rows - W + 1),
    ).reshape(rows, 1)
    own = project_keys_values(hidden, w_key, w_value)
    far = [lax.ppermute(x, "ctx", ahead) for x in own]
    queries = jnp.dot(hidden, w_query, preferred_element_type=jnp.float32).astype(jnp.bfloat16)
    d_queries, gradients = [], []
    for h in range(heads):
        near = lax.ppermute(jnp.where(odd, far[h], own[h]), "ctx", swap)
        dq, gfar, gnear, gown = attend(h, queries, cotangent, far[h], near, own[h], low)
        swapped = lax.ppermute(gnear, "ctx", swap)
        passed = jnp.where(odd, gfar + swapped, gfar)
        returned = lax.ppermute(passed, "ctx", behind)
        total = gown + returned.astype(jnp.float32)
        total = total + jnp.where(odd, 0.0, swapped.astype(jnp.float32))
        d_queries.append(dq)
        gradients.append(total.astype(jnp.bfloat16))

    parts = 3
    chunk = rows // planes
    finished = []
    for part in range(parts):
        mine = back_project(*d_queries, *gradients, w_query, w_key, w_value, part, parts)

        def take(index):
            index = jnp.clip(index, 0, planes - 1)
            return lax.dynamic_slice_in_dim(mine, index * chunk, chunk, 0)

        right = left = None
        for step in range(planes - 1):
            rightward = take(planes - 1 - step + plane)
            leftward = take(step + plane - (planes - 1))
            if step > 0:
                rightward = (rightward.astype(jnp.float32) + right).astype(jnp.bfloat16)
                leftward = (leftward.astype(jnp.float32) + left).astype(jnp.bfloat16)
            right = lax.ppermute(
                rightward, "head", [(i, i + 1) for i in range(step + 1)]
            ).astype(jnp.float32)
            left = lax.ppermute(
                leftward, "head", [(planes - 1 - i, planes - 2 - i) for i in range(step + 1)]
            ).astype(jnp.float32)
        finished.append(take(plane).astype(jnp.float32) + right + left)
    return jnp.concatenate(finished, axis=1)


def solution(mesh):
    in_specs = (
        P("ctx", None),
        P(None, "head"),
        P(None, "head"),
        P(None, "head"),
        P("ctx", "head"),
        P("ctx"),
    )
    out_specs = P(("ctx", "head"), None)
    return jax.shard_map(shards, mesh=mesh, in_specs=in_specs, out_specs=out_specs, check_vma=False)
```

```python
import functools

import jax
import jax.numpy as jnp
from jax import lax
from jax.experimental import pallas as pl
from jax.experimental.pallas import tpu as pltpu
from jax.sharding import PartitionSpec as P

HEAD_SIZE = 128
W = 1024
HALO = 2
SCALE = 168.0 ** (-0.5)
LOG2E = 1.4426950408889634
BLOCK = 128
MASKED = -1e30
MIB = 1024 * 1024
KV_CHUNKS = ((0, 768), (768, 1536), (2304, 1536), (3840, 1024), (4864, 512))
Q_CHUNKS = ((0, 768), (768, 1536), (2304, 1536), (3840, 1536))
PIECES = ((0, 768, 768), (768, 1536, 768), (2304, 1536, 768), (3840, 1536, 768))
PROJECT_LIMIT = 18 * MIB
ATTENTION_LIMIT = 24 * MIB
BACK_LIMIT = 20 * MIB

NT = (((1,), (1,)), ((), ()))


def column_chunks(chunks, hidden_ref, hidden_buf, pairs, sems):
    copies = []
    for at, (first, size) in enumerate(chunks):
        span = pl.ds(first, size)
        group = [pltpu.make_async_copy(hidden_ref.at[:, span], hidden_buf.at[:, span], sems.at[at, 0])]
        for n, (ref, buf) in enumerate(pairs):
            group.append(
                pltpu.make_async_copy(ref.at[span, :], buf.at[span, :], sems.at[at, n + 1])
            )
        for copy in group:
            copy.start()
        copies.append(group)
    return copies


def accumulate(chunks, copies, hidden_buf, bufs):
    totals = [None] * len(bufs)
    for at, (first, size) in enumerate(chunks):
        for copy in copies[at]:
            copy.wait()
        span = slice(first, first + size)
        part = hidden_buf[:, span]
        for n, buf in enumerate(bufs):
            dot = jnp.dot(part, buf[span, :], preferred_element_type=jnp.float32)
            totals[n] = dot if at == 0 else totals[n] + dot
    return totals


def project_kernel(hidden_ref, wk_ref, wv_ref, *refs):
    heads = wk_ref.shape[1] // HEAD_SIZE
    outs, (hidden_buf, k_buf, v_buf, sems) = refs[:heads], refs[heads:]
    copies = column_chunks(
        KV_CHUNKS, hidden_ref, hidden_buf, ((wk_ref, k_buf), (wv_ref, v_buf)), sems
    )
    keys, values = accumulate(KV_CHUNKS, copies, hidden_buf, (k_buf, v_buf))
    for head, out in enumerate(outs):
        cols = slice(head * HEAD_SIZE, (head + 1) * HEAD_SIZE)
        out[:, :HEAD_SIZE] = keys[:, cols].astype(out.dtype)
        out[:, HEAD_SIZE:] = values[:, cols].astype(out.dtype)


def project_keys_values(hidden, wk, wv):
    rows, depth = hidden.shape
    width = wk.shape[1]
    heads = width // HEAD_SIZE
    hbm = pl.BlockSpec(memory_space=pl.ANY)
    vmem = pl.BlockSpec(memory_space=pltpu.VMEM)
    return pl.pallas_call(
        project_kernel,
        in_specs=[hbm] * 3,
        out_specs=[vmem] * heads,
        out_shape=[jax.ShapeDtypeStruct((rows, 2 * HEAD_SIZE), jnp.bfloat16)] * heads,
        scratch_shapes=[
            pltpu.VMEM((rows, depth), jnp.bfloat16),
            pltpu.VMEM((depth, width), jnp.bfloat16),
            pltpu.VMEM((depth, width), jnp.bfloat16),
            pltpu.SemaphoreType.DMA((len(KV_CHUNKS), 3)),
        ],
        compiler_params=pltpu.CompilerParams(vmem_limit_bytes=PROJECT_LIMIT),
        cost_estimate=pl.CostEstimate(
            flops=4 * rows * depth * width,
            bytes_accessed=2 * (rows * depth + 2 * depth * width),
            transcendentals=0,
        ),
        name="project_kv",
    )(hidden, wk, wv)


def query_kernel(hidden_ref, wq_ref, out_ref, hidden_buf, q_buf, sems):
    copies = column_chunks(Q_CHUNKS, hidden_ref, hidden_buf, ((wq_ref, q_buf),), sems)
    (queries,) = accumulate(Q_CHUNKS, copies, hidden_buf, (q_buf,))
    out_ref[...] = queries.astype(out_ref.dtype)


def project_queries(hidden, wq):
    rows, depth = hidden.shape
    width = wq.shape[1]
    hbm = pl.BlockSpec(memory_space=pl.ANY)
    return pl.pallas_call(
        query_kernel,
        in_specs=[hbm] * 2,
        out_specs=pl.BlockSpec(memory_space=pltpu.VMEM),
        out_shape=jax.ShapeDtypeStruct((rows, width), jnp.bfloat16),
        scratch_shapes=[
            pltpu.VMEM((rows, depth), jnp.bfloat16),
            pltpu.VMEM((depth, width), jnp.bfloat16),
            pltpu.SemaphoreType.DMA((len(Q_CHUNKS), 2)),
        ],
        compiler_params=pltpu.CompilerParams(vmem_limit_bytes=PROJECT_LIMIT),
        cost_estimate=pl.CostEstimate(
            flops=2 * rows * depth * width,
            bytes_accessed=2 * (rows * depth + depth * width),
            transcendentals=0,
        ),
        name="project_q",
    )(hidden, wq)


def attention_kernel(
    q_ref, do_ref, far_ref, near_ref, own_ref, low_ref,
    dq_ref, gfar_ref, gnear_ref, gown_ref,
    k_ref, v_ref, dkt_ref, dvt_ref,
):
    rows = q_ref.shape[0]
    window = W + BLOCK
    for at, ref in enumerate((far_ref, near_ref, own_ref)):
        k_ref[at * rows : (at + 1) * rows, :] = ref[:, :HEAD_SIZE]
        v_ref[at * rows : (at + 1) * rows, :] = ref[:, HEAD_SIZE:]
    dkt_ref[...] = jnp.zeros_like(dkt_ref)
    dvt_ref[...] = jnp.zeros_like(dvt_ref)
    for block in range(rows // BLOCK):
        at = slice(block * BLOCK, (block + 1) * BLOCK)
        span = slice(block * BLOCK, block * BLOCK + window)
        q = jnp.concatenate([q_ref[at, :HEAD_SIZE], q_ref[at, HEAD_SIZE:]], axis=0)
        do = jnp.concatenate([do_ref[at, :HEAD_SIZE], do_ref[at, HEAD_SIZE:]], axis=0)
        k = k_ref[span, :]
        v = v_ref[span, :]
        low = low_ref[at, :]
        low = jnp.concatenate([low, low], axis=0) - block * BLOCK
        scores = lax.dot_general(q, k, NT, preferred_element_type=jnp.float32)
        col = lax.broadcasted_iota(jnp.int32, scores.shape, 1)
        row = lax.broadcasted_iota(jnp.int32, scores.shape, 0) & (BLOCK - 1)
        allowed = (col >= low) & (col <= row + W)
        scores = jnp.where(allowed, scores * (SCALE * LOG2E), MASKED)
        top = jnp.max(scores, axis=1, keepdims=True)
        e = jnp.exp2(scores - top)
        inverse = 1.0 / jnp.sum(e, axis=1, keepdims=True)
        probability = e * inverse
        probability_low = probability.astype(jnp.bfloat16)
        d_probs = lax.dot_general(do, v, NT, preferred_element_type=jnp.float32)
        row_dot = jnp.sum(
            probability_low.astype(jnp.float32) * d_probs, axis=1, keepdims=True
        )
        d_scores = (probability * ((d_probs - row_dot) * SCALE)).astype(jnp.bfloat16)
        dq = jnp.dot(d_scores, k, preferred_element_type=jnp.float32).astype(dq_ref.dtype)
        dq_ref[at, :HEAD_SIZE] = dq[:BLOCK]
        dq_ref[at, HEAD_SIZE:] = dq[BLOCK:]
        dkt_ref[:, span] += jnp.dot(q.T, d_scores, preferred_element_type=jnp.float32)
        dvt_ref[:, span] += jnp.dot(do.T, probability_low, preferred_element_type=jnp.float32)
    for at, ref in enumerate((gfar_ref, gnear_ref, gown_ref)):
        part = slice(at * rows, (at + 1) * rows)
        ref[:, :HEAD_SIZE] = dkt_ref[:, part].T.astype(ref.dtype)
        ref[:, HEAD_SIZE:] = dvt_ref[:, part].T.astype(ref.dtype)


def attend(head, queries, cotangent, far, near, own, low):
    rows = queries.shape[0]
    pair = 2 * HEAD_SIZE
    covered = (HALO + 1) * rows
    whole = pl.BlockSpec((rows, pair), lambda i: (0, 0))
    column = pl.BlockSpec((rows, pair), lambda i: (0, head))
    work = 2 * rows * (W + BLOCK) * HEAD_SIZE
    return pl.pallas_call(
        attention_kernel,
        grid=(1,),
        in_specs=[column, column, whole, whole, whole, pl.BlockSpec((rows, 1), lambda i: (0, 0))],
        out_specs=[whole] * 4,
        out_shape=[
            jax.ShapeDtypeStruct((rows, pair), jnp.bfloat16),
            jax.ShapeDtypeStruct((rows, pair), jnp.bfloat16),
            jax.ShapeDtypeStruct((rows, pair), jnp.bfloat16),
            jax.ShapeDtypeStruct((rows, pair), jnp.float32),
        ],
        scratch_shapes=[
            pltpu.VMEM((covered, HEAD_SIZE), jnp.bfloat16),
            pltpu.VMEM((covered, HEAD_SIZE), jnp.bfloat16),
            pltpu.VMEM((HEAD_SIZE, covered), jnp.float32),
            pltpu.VMEM((HEAD_SIZE, covered), jnp.float32),
        ],
        compiler_params=pltpu.CompilerParams(vmem_limit_bytes=ATTENTION_LIMIT),
        cost_estimate=pl.CostEstimate(
            flops=16 * work, bytes_accessed=16 * rows * pair, transcendentals=work // HEAD_SIZE
        ),
        name="attention",
    )(queries, cotangent, far, near, own, low)


def nt(x, w):
    return lax.dot_general(x, w, NT, preferred_element_type=jnp.float32)


def back_kernel(dq0_ref, dq1_ref, g0_ref, g1_ref, wq_ref, wk_ref, wv_ref, out_ref):
    size = HEAD_SIZE
    dk = jnp.concatenate([g0_ref[:, :size], g1_ref[:, :size]], axis=1)
    dv = jnp.concatenate([g0_ref[:, size:], g1_ref[:, size:]], axis=1)
    dq = jnp.concatenate([dq0_ref[...], dq1_ref[...]], axis=1)
    total = nt(dq, wq_ref[...]) + nt(dk, wk_ref[...]) + nt(dv, wv_ref[...])
    out_ref[...] = total.astype(out_ref.dtype)


def back_project(dq0, dq1, g0, g1, wq, wk, wv, first, columns, tile):
    rows = dq0.shape[0]
    base = first // tile
    return pl.pallas_call(
        back_kernel,
        grid=(columns // tile,),
        in_specs=[pl.BlockSpec(x.shape, lambda j: (0, 0)) for x in (dq0, dq1, g0, g1)]
        + [pl.BlockSpec((tile, w.shape[1]), lambda j: (base + j, 0)) for w in (wq, wk, wv)],
        out_specs=pl.BlockSpec((rows, tile), lambda j: (0, j)),
        out_shape=jax.ShapeDtypeStruct((rows, columns), jnp.bfloat16),
        compiler_params=pltpu.CompilerParams(vmem_limit_bytes=BACK_LIMIT),
        cost_estimate=pl.CostEstimate(
            flops=2 * rows * columns * 1024,
            bytes_accessed=2 * columns * (1024 + rows),
            transcendentals=0,
        ),
        name="back_project",
    )(dq0, dq1, g0, g1, wq, wk, wv)


def add(a, b):
    return (a.astype(jnp.float32) + b.astype(jnp.float32)).astype(jnp.bfloat16)


def shards(hidden, w_query, w_key, w_value, cotangent, doc_start):
    rows = hidden.shape[0]
    contexts = lax.axis_size("ctx")
    planes = lax.axis_size("head")
    ctx = lax.axis_index("ctx")
    plane = lax.axis_index("head")
    odd = (ctx % 2) == 1
    outer = (plane == 0) | (plane == planes - 1)
    heads = w_key.shape[1] // HEAD_SIZE
    chunk = rows // planes
    swap = [(i, i ^ 1) for i in range(contexts)]
    ahead = [(i, i + 2) for i in range(contexts - 2)]
    behind = [(i + 2, i) for i in range(contexts - 2)]
    inward = [(0, 1), (3, 2)]
    middle = [(1, 2), (2, 1)]
    outward = [(1, 0), (2, 3)]
    hidden, *weights = (
        pltpu.with_memory_space_constraint(x, pltpu.HBM)
        for x in (hidden, w_query, w_key, w_value)
    )

    low = jnp.maximum(
        doc_start - ctx * rows + HALO * rows,
        jnp.arange(rows, dtype=jnp.int32) + (HALO * rows - W + 1),
    ).reshape(rows, 1)
    own = project_keys_values(hidden, *weights[1:])
    far = [lax.ppermute(x, "ctx", ahead) for x in own]
    queries = project_queries(hidden, weights[0])
    d_queries, gradients = [], []
    for h in range(heads):
        near = lax.ppermute(jnp.where(odd, far[h], own[h]), "ctx", swap)
        dq, gfar, gnear, gown = attend(h, queries, cotangent, far[h], near, own[h], low)
        swapped = lax.ppermute(gnear, "ctx", swap)
        passed = jnp.where(odd, add(gfar, swapped), gfar)
        if h + 1 < heads:
            passed, queries = lax.optimization_barrier((passed, queries))
        returned = lax.ppermute(passed, "ctx", behind)
        total = gown + returned.astype(jnp.float32)
        total = total + jnp.where(odd, 0.0, swapped.astype(jnp.float32))
        d_queries.append(dq)
        gradients.append(total.astype(jnp.bfloat16))

    def take(array, index):
        return lax.dynamic_slice_in_dim(array, jnp.clip(index, 0, planes - 1) * chunk, chunk, 0)

    low_side = plane < 2

    def toward(array, low_index, high_index):
        return take(array, jnp.where(low_side, low_index, high_index))

    blocks = [back_project(*d_queries, *gradients, *weights, *piece) for piece in PIECES]
    r0 = [lax.ppermute(toward(block, 3, 0), "head", inward) for block in blocks]
    r1, m1 = [], []
    for n, block in enumerate(blocks):
        m1.append(lax.ppermute(add(toward(block, 3, 0), r0[n]), "head", middle))
        payload, _ = lax.optimization_barrier((toward(block, 2, 1), r0[n]))
        r1.append(lax.ppermute(payload, "head", inward))
    r2, m2 = [], []
    for n, block in enumerate(blocks):
        m2.append(lax.ppermute(add(toward(block, 2, 1), r1[n]), "head", middle))
        payload = jnp.where(outer, toward(block, 1, 2), add(toward(block, 0, 3), m1[n]))
        payload, _ = lax.optimization_barrier((payload, r1[n]))
        r2.append(lax.ppermute(payload, "head", inward + outward))
    return jnp.concatenate(
        [
            sum(part.astype(jnp.float32) for part in (take(block, plane), *parts))
            for block, *parts in zip(blocks, m2, r2)
        ],
        axis=1,
    )


def solution(mesh):
    in_specs = (
        P("ctx", None),
        P(None, "head"),
        P(None, "head"),
        P(None, "head"),
        P("ctx", "head"),
        P("ctx"),
    )
    out_specs = P(("ctx", "head"), None)
    return jax.shard_map(shards, mesh=mesh, in_specs=in_specs, out_specs=out_specs, check_vma=False)
```

```python
import functools

import jax
import jax.numpy as jnp
from jax import lax
from jax.experimental import pallas as pl
from jax.experimental.pallas import tpu as pltpu
from jax.sharding import PartitionSpec as P

HEAD_SIZE = 128
W = 1024
HALO = 2
SCALE = 168.0 ** (-0.5)
LOG2E = 1.4426950408889634
BLOCK = 128
MASKED = -1e30
MIB = 1024 * 1024
KV_CHUNKS = ((0, 768), (768, 1536), (2304, 1536), (3840, 1024), (4864, 512))
Q_CHUNKS = ((0, 768), (768, 1536), (2304, 1536), (3840, 1536))
TILE = 768
PIECES = ((0, 768), (768, 2304), (3072, 2304))
OUTER_DEPTH, MIDDLE_DEPTH = 3, 2
PROJECT_LIMIT = 18 * MIB
ATTENTION_LIMIT = 14 * MIB
BACK_LIMIT = 20 * MIB

NT = (((1,), (1,)), ((), ()))


def column_chunks(chunks, hidden_ref, hidden_buf, pairs, sems):
    copies = []
    for at, (first, size) in enumerate(chunks):
        span = pl.ds(first, size)
        group = [pltpu.make_async_copy(hidden_ref.at[:, span], hidden_buf.at[:, span], sems.at[at, 0])]
        for n, (ref, buf) in enumerate(pairs):
            group.append(
                pltpu.make_async_copy(ref.at[span, :], buf.at[span, :], sems.at[at, n + 1])
            )
        for copy in group:
            copy.start()
        copies.append(group)
    return copies


def accumulate(chunks, copies, hidden_buf, bufs):
    totals = [None] * len(bufs)
    for at, (first, size) in enumerate(chunks):
        for copy in copies[at]:
            copy.wait()
        span = slice(first, first + size)
        part = hidden_buf[:, span]
        for n, buf in enumerate(bufs):
            dot = jnp.dot(part, buf[span, :], preferred_element_type=jnp.float32)
            totals[n] = dot if at == 0 else totals[n] + dot
    return totals


def project_kernel(hidden_ref, wk_ref, wv_ref, *refs):
    heads = wk_ref.shape[1] // HEAD_SIZE
    outs, (hidden_buf, k_buf, v_buf, sems) = refs[:heads], refs[heads:]
    copies = column_chunks(
        KV_CHUNKS, hidden_ref, hidden_buf, ((wk_ref, k_buf), (wv_ref, v_buf)), sems
    )
    keys, values = accumulate(KV_CHUNKS, copies, hidden_buf, (k_buf, v_buf))
    for head, out in enumerate(outs):
        cols = slice(head * HEAD_SIZE, (head + 1) * HEAD_SIZE)
        out[:, :HEAD_SIZE] = keys[:, cols].astype(out.dtype)
        out[:, HEAD_SIZE:] = values[:, cols].astype(out.dtype)


def project_keys_values(hidden, wk, wv):
    rows, depth = hidden.shape
    width = wk.shape[1]
    heads = width // HEAD_SIZE
    hbm = pl.BlockSpec(memory_space=pl.ANY)
    vmem = pl.BlockSpec(memory_space=pltpu.VMEM)
    return pl.pallas_call(
        project_kernel,
        in_specs=[hbm] * 3,
        out_specs=[vmem] * heads,
        out_shape=[jax.ShapeDtypeStruct((rows, 2 * HEAD_SIZE), jnp.bfloat16)] * heads,
        scratch_shapes=[
            pltpu.VMEM((rows, depth), jnp.bfloat16),
            pltpu.VMEM((depth, width), jnp.bfloat16),
            pltpu.VMEM((depth, width), jnp.bfloat16),
            pltpu.SemaphoreType.DMA((len(KV_CHUNKS), 3)),
        ],
        compiler_params=pltpu.CompilerParams(vmem_limit_bytes=PROJECT_LIMIT),
        cost_estimate=pl.CostEstimate(
            flops=4 * rows * depth * width,
            bytes_accessed=2 * (rows * depth + 2 * depth * width),
            transcendentals=0,
        ),
        name="project_kv",
    )(hidden, wk, wv)


def query_kernel(hidden_ref, wq_ref, out_ref, hidden_buf, q_buf, sems):
    copies = column_chunks(Q_CHUNKS, hidden_ref, hidden_buf, ((wq_ref, q_buf),), sems)
    (queries,) = accumulate(Q_CHUNKS, copies, hidden_buf, (q_buf,))
    out_ref[...] = queries.astype(out_ref.dtype)


def project_queries(hidden, wq):
    rows, depth = hidden.shape
    width = wq.shape[1]
    hbm = pl.BlockSpec(memory_space=pl.ANY)
    return pl.pallas_call(
        query_kernel,
        in_specs=[hbm] * 2,
        out_specs=pl.BlockSpec(memory_space=pltpu.VMEM),
        out_shape=jax.ShapeDtypeStruct((rows, width), jnp.bfloat16),
        scratch_shapes=[
            pltpu.VMEM((rows, depth), jnp.bfloat16),
            pltpu.VMEM((depth, width), jnp.bfloat16),
            pltpu.SemaphoreType.DMA((len(Q_CHUNKS), 2)),
        ],
        compiler_params=pltpu.CompilerParams(vmem_limit_bytes=PROJECT_LIMIT),
        cost_estimate=pl.CostEstimate(
            flops=2 * rows * depth * width,
            bytes_accessed=2 * (rows * depth + depth * width),
            transcendentals=0,
        ),
        name="project_q",
    )(hidden, wq)


def attention_kernel(
    q_ref, do_ref, far_ref, near_ref, own_ref, low_ref,
    dq_ref, gfar_ref, gnear_ref, gown_ref,
    k_ref, v_ref, dkt_ref, dvt_ref,
):
    rows = q_ref.shape[0]
    window = W + BLOCK
    for at, ref in enumerate((far_ref, near_ref, own_ref)):
        k_ref[at * rows : (at + 1) * rows, :] = ref[:, :HEAD_SIZE]
        v_ref[at * rows : (at + 1) * rows, :] = ref[:, HEAD_SIZE:]
    dkt_ref[...] = jnp.zeros_like(dkt_ref)
    dvt_ref[...] = jnp.zeros_like(dvt_ref)
    for block in range(rows // BLOCK):
        at = slice(block * BLOCK, (block + 1) * BLOCK)
        span = slice(block * BLOCK, block * BLOCK + window)
        q = jnp.concatenate([q_ref[at, :HEAD_SIZE], q_ref[at, HEAD_SIZE:]], axis=0)
        do = jnp.concatenate([do_ref[at, :HEAD_SIZE], do_ref[at, HEAD_SIZE:]], axis=0)
        k = k_ref[span, :]
        v = v_ref[span, :]
        low = low_ref[at, :]
        low = jnp.concatenate([low, low], axis=0) - block * BLOCK
        scores = lax.dot_general(q, k, NT, preferred_element_type=jnp.float32)
        col = lax.broadcasted_iota(jnp.int32, scores.shape, 1)
        row = lax.broadcasted_iota(jnp.int32, scores.shape, 0) & (BLOCK - 1)
        allowed = (col >= low) & (col <= row + W)
        scores = jnp.where(allowed, scores * (SCALE * LOG2E), MASKED)
        top = jnp.max(scores, axis=1, keepdims=True)
        e = jnp.exp2(scores - top)
        inverse = 1.0 / jnp.sum(e, axis=1, keepdims=True)
        probability = e * inverse
        probability_low = probability.astype(jnp.bfloat16)
        d_probs = lax.dot_general(do, v, NT, preferred_element_type=jnp.float32)
        row_dot = jnp.sum(
            probability_low.astype(jnp.float32) * d_probs, axis=1, keepdims=True
        )
        d_scores = (probability * ((d_probs - row_dot) * SCALE)).astype(jnp.bfloat16)
        dq = jnp.dot(d_scores, k, preferred_element_type=jnp.float32).astype(dq_ref.dtype)
        dq_ref[at, :HEAD_SIZE] = dq[:BLOCK]
        dq_ref[at, HEAD_SIZE:] = dq[BLOCK:]
        dkt_ref[:, span] += jnp.dot(q.T, d_scores, preferred_element_type=jnp.float32)
        dvt_ref[:, span] += jnp.dot(do.T, probability_low, preferred_element_type=jnp.float32)
    for at, ref in enumerate((gfar_ref, gnear_ref, gown_ref)):
        part = slice(at * rows, (at + 1) * rows)
        ref[:, :HEAD_SIZE] = dkt_ref[:, part].T.astype(ref.dtype)
        ref[:, HEAD_SIZE:] = dvt_ref[:, part].T.astype(ref.dtype)


def attend(head, queries, cotangent, far, near, own, low):
    rows = queries.shape[0]
    pair = 2 * HEAD_SIZE
    covered = (HALO + 1) * rows
    whole = pl.BlockSpec((rows, pair), lambda i: (0, 0))
    column = pl.BlockSpec((rows, pair), lambda i: (0, head))
    work = 2 * rows * (W + BLOCK) * HEAD_SIZE
    return pl.pallas_call(
        attention_kernel,
        grid=(1,),
        in_specs=[column, column, whole, whole, whole, pl.BlockSpec((rows, 1), lambda i: (0, 0))],
        out_specs=[whole] * 4,
        out_shape=[
            jax.ShapeDtypeStruct((rows, pair), jnp.bfloat16),
            jax.ShapeDtypeStruct((rows, pair), jnp.bfloat16),
            jax.ShapeDtypeStruct((rows, pair), jnp.bfloat16),
            jax.ShapeDtypeStruct((rows, pair), jnp.float32),
        ],
        scratch_shapes=[
            pltpu.VMEM((covered, HEAD_SIZE), jnp.bfloat16),
            pltpu.VMEM((covered, HEAD_SIZE), jnp.bfloat16),
            pltpu.VMEM((HEAD_SIZE, covered), jnp.float32),
            pltpu.VMEM((HEAD_SIZE, covered), jnp.float32),
        ],
        compiler_params=pltpu.CompilerParams(vmem_limit_bytes=ATTENTION_LIMIT),
        cost_estimate=pl.CostEstimate(
            flops=16 * work, bytes_accessed=16 * rows * pair, transcendentals=work // HEAD_SIZE
        ),
        name="attention",
    )(queries, cotangent, far, near, own, low)


def nt(x, w):
    return lax.dot_general(x, w, NT, preferred_element_type=jnp.float32)


def back_kernel(spans, place_ref, dq0_ref, dq1_ref, g0_ref, g1_ref, wq_ref, wk_ref, wv_ref, *refs):
    outs, buf = refs[:-1], refs[-1]
    count = len(outs) // len(spans)
    size = HEAD_SIZE
    pair = 2 * size
    step = pl.program_id(0)

    @pl.when(step == 0)
    def _():
        for n in range(count):
            span = pl.ds(pl.multiple_of(place_ref[n] * size, size), size)
            here = slice(n * size, (n + 1) * size)
            buf[here, :pair] = dq0_ref[span, :]
            buf[here, pair : 2 * pair] = dq1_ref[span, :]
            for at, ref in enumerate((g0_ref, g1_ref)):
                rows = ref[span, :]
                buf[here, 2 * pair + at * size : 2 * pair + (at + 1) * size] = rows[:, :size]
                buf[here, 3 * pair + at * size : 3 * pair + (at + 1) * size] = rows[:, size:]

    total = nt(buf[:, : 2 * pair], wq_ref[...]) + nt(buf[:, 2 * pair : 3 * pair], wk_ref[...])
    total = (total + nt(buf[:, 3 * pair :], wv_ref[...])).astype(jnp.bfloat16)
    for at, (first, steps) in enumerate(spans):

        @pl.when((step >= first) & (step < first + steps))
        def _():
            for n in range(count):
                outs[at * count + n][...] = total[n * size : (n + 1) * size]


def back_project(chunks, count, grads, weights, pieces):
    base = pieces[0][0] // TILE
    spans = [(first // TILE - base, columns // TILE) for first, columns in pieces]
    columns = sum(columns for _, columns in pieces)
    rows = HEAD_SIZE

    def out_spec(first, steps):
        return pl.BlockSpec((rows, TILE), lambda j, place: (0, jnp.clip(j - first, 0, steps - 1)))

    grid_spec = pltpu.PrefetchScalarGridSpec(
        num_scalar_prefetch=1,
        grid=(columns // TILE,),
        in_specs=[pl.BlockSpec(x.shape, lambda j, place: (0, 0)) for x in grads]
        + [pl.BlockSpec((TILE, w.shape[1]), lambda j, place: (base + j, 0)) for w in weights],
        out_specs=[out_spec(*span) for span in spans for _ in range(count)],
        scratch_shapes=[pltpu.VMEM((count * rows, 1024), jnp.bfloat16)],
    )
    outs = pl.pallas_call(
        functools.partial(back_kernel, spans),
        grid_spec=grid_spec,
        out_shape=[
            jax.ShapeDtypeStruct((rows, columns), jnp.bfloat16)
            for _, columns in pieces
            for _ in range(count)
        ],
        compiler_params=pltpu.CompilerParams(vmem_limit_bytes=BACK_LIMIT),
        cost_estimate=pl.CostEstimate(
            flops=2 * count * rows * columns * 1024,
            bytes_accessed=2 * columns * (1024 + count * rows),
            transcendentals=0,
        ),
        name="back_project",
    )(chunks, *grads, *weights)
    return [outs[at * count : (at + 1) * count] for at in range(len(pieces))]


def add(a, b):
    return (a.astype(jnp.float32) + b.astype(jnp.float32)).astype(jnp.bfloat16)


def shards(hidden, w_query, w_key, w_value, cotangent, doc_start):
    rows = hidden.shape[0]
    contexts = lax.axis_size("ctx")
    planes = lax.axis_size("head")
    ctx = lax.axis_index("ctx")
    plane = lax.axis_index("head")
    odd = (ctx % 2) == 1
    outer = (plane == 0) | (plane == planes - 1)
    heads = w_key.shape[1] // HEAD_SIZE
    chunk = rows // planes
    swap = [(i, i ^ 1) for i in range(contexts)]
    ahead = [(i, i + 2) for i in range(contexts - 2)]
    behind = [(i + 2, i) for i in range(contexts - 2)]
    inward = [(0, 1), (3, 2)]
    middle = [(1, 2), (2, 1)]
    outward = [(1, 0), (2, 3)]
    hidden, *weights = (
        pltpu.with_memory_space_constraint(x, pltpu.HBM)
        for x in (hidden, w_query, w_key, w_value)
    )

    low = jnp.maximum(
        doc_start - ctx * rows + HALO * rows,
        jnp.arange(rows, dtype=jnp.int32) + (HALO * rows - W + 1),
    ).reshape(rows, 1)
    own = project_keys_values(hidden, *weights[1:])
    far = [lax.ppermute(x, "ctx", ahead) for x in own]
    queries = project_queries(hidden, weights[0])
    far[0], queries = lax.optimization_barrier((far[0], queries))
    d_queries, gradients, waiting = [], [], []

    def finish():
        gown, swapped = waiting.pop()
        total = gown + returned.astype(jnp.float32)
        total = total + jnp.where(odd, 0.0, swapped.astype(jnp.float32))
        gradients.append(total.astype(jnp.bfloat16))

    for h in range(heads):
        near = lax.ppermute(jnp.where(odd, far[h], own[h]), "ctx", swap)
        dq, gfar, gnear, gown = attend(h, queries, cotangent, far[h], near, own[h], low)
        if h > 0:
            gnear, returned = lax.optimization_barrier((gnear, returned))
            finish()
        swapped = lax.ppermute(gnear, "ctx", swap)
        passed = jnp.where(odd, add(gfar, swapped), gfar)
        if h + 1 < heads:
            passed, queries = lax.optimization_barrier((passed, queries))
        returned = lax.ppermute(passed, "ctx", behind)
        d_queries.append(dq)
        waiting.append((gown, swapped))
    finish()

    low_side = plane < 2

    side = jnp.where(low_side, 3, 0)
    step = jnp.where(low_side, -1, 1)
    order = [(side + step * n).astype(jnp.int32) for n in range(planes)]
    last = jnp.where(outer, order[2], order[3])
    home = jnp.where(outer, order[3], order[2])
    grads = (*d_queries, *gradients)
    edge = [
        back_project(order[0].reshape(1), 1, grads, weights, [piece])[0][0] for piece in PIECES
    ]
    sent_outer, sent_middle = [], []

    def send(payload, pairs, sent, depth):
        if len(sent) >= depth:
            payload, _ = lax.optimization_barrier((payload, sent[-depth]))
        sent.append(lax.ppermute(payload, "head", pairs))
        return sent[-1]

    def send_outer(payload, pairs):
        return send(payload, pairs, sent_outer, OUTER_DEPTH)

    def send_middle(payload):
        return send(payload, middle, sent_middle, MIDDLE_DEPTH)

    r0 = [send_outer(block, inward) for block in edge]
    *grads, _ = lax.optimization_barrier((*grads, r0[0]))
    others = jnp.stack([order[1], last, home])
    blocks = back_project(others, 3, grads, weights, PIECES)
    m1 = [send_middle(add(block, r)) for block, r in zip(edge, r0)]
    r1 = [send_outer(block[0], inward) for block in blocks]
    m2 = [send_middle(add(block[0], r)) for block, r in zip(blocks, r1)]
    r2 = [send_outer(add(block[1], m), inward + outward) for block, m in zip(blocks, m1)]
    blocks = [block[2] for block in blocks]
    return jnp.concatenate(
        [
            sum(part.astype(jnp.float32) for part in (block, *parts))
            for block, *parts in zip(blocks, m2, r2)
        ],
        axis=1,
    )


def solution(mesh):
    in_specs = (
        P("ctx", None),
        P(None, "head"),
        P(None, "head"),
        P(None, "head"),
        P("ctx", "head"),
        P("ctx"),
    )
    out_specs = P(("ctx", "head"), None)
    return jax.shard_map(shards, mesh=mesh, in_specs=in_specs, out_specs=out_specs, check_vma=False)
```

```python
import functools

import jax
import jax.numpy as jnp
from jax import lax
from jax.experimental import pallas as pl
from jax.experimental.pallas import tpu as pltpu
from jax.sharding import PartitionSpec as P

HEAD_SIZE = 128
W = 1024
HALO = 2
SCALE = 168.0 ** (-0.5)
LOG2E = 1.4426950408889634
BLOCK = 128
MASKED = -1e30
MIB = 1024 * 1024
KV_CHUNKS = ((0, 768), (768, 1536), (2304, 1536), (3840, 1024), (4864, 512))
Q_CHUNKS = ((0, 768), (768, 1536), (2304, 1536), (3840, 1536))
TILE = 768
PIECES = ((0, 1536), (1536, 1536), (3072, 2304))
OUTER_DEPTH, MIDDLE_DEPTH = 3, 2
PROJECT_LIMIT = 18 * MIB
ATTENTION_LIMIT = 14 * MIB
BACK_LIMIT = 20 * MIB

NT = (((1,), (1,)), ((), ()))


def column_chunks(chunks, hidden_ref, hidden_buf, pairs, sems):
    copies = []
    for at, (first, size) in enumerate(chunks):
        span = pl.ds(first, size)
        group = [pltpu.make_async_copy(hidden_ref.at[:, span], hidden_buf.at[:, span], sems.at[at, 0])]
        for n, (ref, buf) in enumerate(pairs):
            group.append(
                pltpu.make_async_copy(ref.at[span, :], buf.at[span, :], sems.at[at, n + 1])
            )
        for copy in group:
            copy.start()
        copies.append(group)
    return copies


def accumulate(chunks, copies, hidden_buf, bufs):
    totals = [None] * len(bufs)
    for at, (first, size) in enumerate(chunks):
        for copy in copies[at]:
            copy.wait()
        span = slice(first, first + size)
        part = hidden_buf[:, span]
        for n, buf in enumerate(bufs):
            dot = jnp.dot(part, buf[span, :], preferred_element_type=jnp.float32)
            totals[n] = dot if at == 0 else totals[n] + dot
    return totals


def project_kernel(hidden_ref, wk_ref, wv_ref, *refs):
    heads = wk_ref.shape[1] // HEAD_SIZE
    outs, (hidden_buf, k_buf, v_buf, sems) = refs[:heads], refs[heads:]
    copies = column_chunks(
        KV_CHUNKS, hidden_ref, hidden_buf, ((wk_ref, k_buf), (wv_ref, v_buf)), sems
    )
    keys, values = accumulate(KV_CHUNKS, copies, hidden_buf, (k_buf, v_buf))
    for head, out in enumerate(outs):
        cols = slice(head * HEAD_SIZE, (head + 1) * HEAD_SIZE)
        out[:, :HEAD_SIZE] = keys[:, cols].astype(out.dtype)
        out[:, HEAD_SIZE:] = values[:, cols].astype(out.dtype)


def project_keys_values(hidden, wk, wv):
    rows, depth = hidden.shape
    width = wk.shape[1]
    heads = width // HEAD_SIZE
    hbm = pl.BlockSpec(memory_space=pl.ANY)
    vmem = pl.BlockSpec(memory_space=pltpu.VMEM)
    return pl.pallas_call(
        project_kernel,
        in_specs=[hbm] * 3,
        out_specs=[vmem] * heads,
        out_shape=[jax.ShapeDtypeStruct((rows, 2 * HEAD_SIZE), jnp.bfloat16)] * heads,
        scratch_shapes=[
            pltpu.VMEM((rows, depth), jnp.bfloat16),
            pltpu.VMEM((depth, width), jnp.bfloat16),
            pltpu.VMEM((depth, width), jnp.bfloat16),
            pltpu.SemaphoreType.DMA((len(KV_CHUNKS), 3)),
        ],
        compiler_params=pltpu.CompilerParams(vmem_limit_bytes=PROJECT_LIMIT),
        cost_estimate=pl.CostEstimate(
            flops=4 * rows * depth * width,
            bytes_accessed=2 * (rows * depth + 2 * depth * width),
            transcendentals=0,
        ),
        name="project_kv",
    )(hidden, wk, wv)


def query_kernel(hidden_ref, wq_ref, out_ref, hidden_buf, q_buf, sems):
    copies = column_chunks(Q_CHUNKS, hidden_ref, hidden_buf, ((wq_ref, q_buf),), sems)
    (queries,) = accumulate(Q_CHUNKS, copies, hidden_buf, (q_buf,))
    out_ref[...] = queries.astype(out_ref.dtype)


def project_queries(hidden, wq):
    rows, depth = hidden.shape
    width = wq.shape[1]
    hbm = pl.BlockSpec(memory_space=pl.ANY)
    return pl.pallas_call(
        query_kernel,
        in_specs=[hbm] * 2,
        out_specs=pl.BlockSpec(memory_space=pltpu.VMEM),
        out_shape=jax.ShapeDtypeStruct((rows, width), jnp.bfloat16),
        scratch_shapes=[
            pltpu.VMEM((rows, depth), jnp.bfloat16),
            pltpu.VMEM((depth, width), jnp.bfloat16),
            pltpu.SemaphoreType.DMA((len(Q_CHUNKS), 2)),
        ],
        compiler_params=pltpu.CompilerParams(vmem_limit_bytes=PROJECT_LIMIT),
        cost_estimate=pl.CostEstimate(
            flops=2 * rows * depth * width,
            bytes_accessed=2 * (rows * depth + depth * width),
            transcendentals=0,
        ),
        name="project_q",
    )(hidden, wq)


def attention_kernel(
    q_ref, do_ref, far_ref, near_ref, own_ref, low_ref,
    dq_ref, gfar_ref, gnear_ref, gown_ref,
    k_ref, v_ref, dkt_ref, dvt_ref,
):
    rows = q_ref.shape[0]
    window = W + BLOCK
    for at, ref in enumerate((far_ref, near_ref, own_ref)):
        k_ref[at * rows : (at + 1) * rows, :] = ref[:, :HEAD_SIZE]
        v_ref[at * rows : (at + 1) * rows, :] = ref[:, HEAD_SIZE:]
    dkt_ref[...] = jnp.zeros_like(dkt_ref)
    dvt_ref[...] = jnp.zeros_like(dvt_ref)
    for block in range(rows // BLOCK):
        at = slice(block * BLOCK, (block + 1) * BLOCK)
        span = slice(block * BLOCK, block * BLOCK + window)
        q = jnp.concatenate([q_ref[at, :HEAD_SIZE], q_ref[at, HEAD_SIZE:]], axis=0)
        do = jnp.concatenate([do_ref[at, :HEAD_SIZE], do_ref[at, HEAD_SIZE:]], axis=0)
        k = k_ref[span, :]
        v = v_ref[span, :]
        low = low_ref[at, :]
        low = jnp.concatenate([low, low], axis=0) - block * BLOCK
        scores = lax.dot_general(q, k, NT, preferred_element_type=jnp.float32)
        col = lax.broadcasted_iota(jnp.int32, scores.shape, 1)
        row = lax.broadcasted_iota(jnp.int32, scores.shape, 0) & (BLOCK - 1)
        allowed = (col >= low) & (col <= row + W)
        scores = jnp.where(allowed, scores * (SCALE * LOG2E), MASKED)
        top = jnp.max(scores, axis=1, keepdims=True)
        e = jnp.exp2(scores - top)
        inverse = 1.0 / jnp.sum(e, axis=1, keepdims=True)
        probability = e * inverse
        probability_low = probability.astype(jnp.bfloat16)
        d_probs = lax.dot_general(do, v, NT, preferred_element_type=jnp.float32)
        row_dot = jnp.sum(
            probability_low.astype(jnp.float32) * d_probs, axis=1, keepdims=True
        )
        d_scores = (probability * ((d_probs - row_dot) * SCALE)).astype(jnp.bfloat16)
        dq = jnp.dot(d_scores, k, preferred_element_type=jnp.float32).astype(dq_ref.dtype)
        dq_ref[at, :HEAD_SIZE] = dq[:BLOCK]
        dq_ref[at, HEAD_SIZE:] = dq[BLOCK:]
        dkt_ref[:, span] += jnp.dot(q.T, d_scores, preferred_element_type=jnp.float32)
        dvt_ref[:, span] += jnp.dot(do.T, probability_low, preferred_element_type=jnp.float32)
    for at, ref in enumerate((gfar_ref, gnear_ref, gown_ref)):
        part = slice(at * rows, (at + 1) * rows)
        ref[:, :HEAD_SIZE] = dkt_ref[:, part].T.astype(ref.dtype)
        ref[:, HEAD_SIZE:] = dvt_ref[:, part].T.astype(ref.dtype)


def attend(head, queries, cotangent, far, near, own, low):
    rows = queries.shape[0]
    pair = 2 * HEAD_SIZE
    covered = (HALO + 1) * rows
    whole = pl.BlockSpec((rows, pair), lambda i: (0, 0))
    column = pl.BlockSpec((rows, pair), lambda i: (0, head))
    work = 2 * rows * (W + BLOCK) * HEAD_SIZE
    return pl.pallas_call(
        attention_kernel,
        grid=(1,),
        in_specs=[column, column, whole, whole, whole, pl.BlockSpec((rows, 1), lambda i: (0, 0))],
        out_specs=[whole] * 4,
        out_shape=[
            jax.ShapeDtypeStruct((rows, pair), jnp.bfloat16),
            jax.ShapeDtypeStruct((rows, pair), jnp.bfloat16),
            jax.ShapeDtypeStruct((rows, pair), jnp.bfloat16),
            jax.ShapeDtypeStruct((rows, pair), jnp.float32),
        ],
        scratch_shapes=[
            pltpu.VMEM((covered, HEAD_SIZE), jnp.bfloat16),
            pltpu.VMEM((covered, HEAD_SIZE), jnp.bfloat16),
            pltpu.VMEM((HEAD_SIZE, covered), jnp.float32),
            pltpu.VMEM((HEAD_SIZE, covered), jnp.float32),
        ],
        compiler_params=pltpu.CompilerParams(vmem_limit_bytes=ATTENTION_LIMIT),
        cost_estimate=pl.CostEstimate(
            flops=16 * work, bytes_accessed=16 * rows * pair, transcendentals=work // HEAD_SIZE
        ),
        name="attention",
    )(queries, cotangent, far, near, own, low)


def nt(x, w):
    return lax.dot_general(x, w, NT, preferred_element_type=jnp.float32)


def back_kernel(spans, place_ref, dq0_ref, dq1_ref, g0_ref, g1_ref, wq_ref, wk_ref, wv_ref, *refs):
    outs, buf = refs[:-1], refs[-1]
    count = len(outs) // len(spans)
    size = HEAD_SIZE
    pair = 2 * size
    step = pl.program_id(0)

    @pl.when(step == 0)
    def _():
        for n in range(count):
            span = pl.ds(pl.multiple_of(place_ref[n] * size, size), size)
            here = slice(n * size, (n + 1) * size)
            buf[here, :pair] = dq0_ref[span, :]
            buf[here, pair : 2 * pair] = dq1_ref[span, :]
            for at, ref in enumerate((g0_ref, g1_ref)):
                rows = ref[span, :]
                buf[here, 2 * pair + at * size : 2 * pair + (at + 1) * size] = rows[:, :size]
                buf[here, 3 * pair + at * size : 3 * pair + (at + 1) * size] = rows[:, size:]

    total = nt(buf[:, : 2 * pair], wq_ref[...]) + nt(buf[:, 2 * pair : 3 * pair], wk_ref[...])
    total = (total + nt(buf[:, 3 * pair :], wv_ref[...])).astype(jnp.bfloat16)
    for at, (first, steps) in enumerate(spans):

        @pl.when((step >= first) & (step < first + steps))
        def _():
            for n in range(count):
                outs[at * count + n][...] = total[n * size : (n + 1) * size]


def back_project(chunks, count, grads, weights, pieces):
    base = pieces[0][0] // TILE
    spans = [(first // TILE - base, columns // TILE) for first, columns in pieces]
    columns = sum(columns for _, columns in pieces)
    rows = HEAD_SIZE

    def out_spec(first, steps):
        return pl.BlockSpec((rows, TILE), lambda j, place: (0, jnp.clip(j - first, 0, steps - 1)))

    grid_spec = pltpu.PrefetchScalarGridSpec(
        num_scalar_prefetch=1,
        grid=(columns // TILE,),
        in_specs=[pl.BlockSpec(x.shape, lambda j, place: (0, 0)) for x in grads]
        + [pl.BlockSpec((TILE, w.shape[1]), lambda j, place: (base + j, 0)) for w in weights],
        out_specs=[out_spec(*span) for span in spans for _ in range(count)],
        scratch_shapes=[pltpu.VMEM((count * rows, 1024), jnp.bfloat16)],
    )
    outs = pl.pallas_call(
        functools.partial(back_kernel, spans),
        grid_spec=grid_spec,
        out_shape=[
            jax.ShapeDtypeStruct((rows, columns), jnp.bfloat16)
            for _, columns in pieces
            for _ in range(count)
        ],
        compiler_params=pltpu.CompilerParams(vmem_limit_bytes=BACK_LIMIT),
        cost_estimate=pl.CostEstimate(
            flops=2 * count * rows * columns * 1024,
            bytes_accessed=2 * columns * (1024 + count * rows),
            transcendentals=0,
        ),
        name="back_project",
    )(chunks, *grads, *weights)
    return [outs[at * count : (at + 1) * count] for at in range(len(pieces))]


def add(a, b):
    return (a.astype(jnp.float32) + b.astype(jnp.float32)).astype(jnp.bfloat16)


def shards(hidden, w_query, w_key, w_value, cotangent, doc_start):
    rows = hidden.shape[0]
    contexts = lax.axis_size("ctx")
    planes = lax.axis_size("head")
    ctx = lax.axis_index("ctx")
    plane = lax.axis_index("head")
    odd = (ctx % 2) == 1
    outer = (plane == 0) | (plane == planes - 1)
    heads = w_key.shape[1] // HEAD_SIZE
    chunk = rows // planes
    swap = [(i, i ^ 1) for i in range(contexts)]
    ahead = [(i, i + 2) for i in range(contexts - 2)]
    behind = [(i + 2, i) for i in range(contexts - 2)]
    inward = [(0, 1), (3, 2)]
    middle = [(1, 2), (2, 1)]
    outward = [(1, 0), (2, 3)]
    hidden, *weights = (
        pltpu.with_memory_space_constraint(x, pltpu.HBM)
        for x in (hidden, w_query, w_key, w_value)
    )

    low = jnp.maximum(
        doc_start - ctx * rows + HALO * rows,
        jnp.arange(rows, dtype=jnp.int32) + (HALO * rows - W + 1),
    ).reshape(rows, 1)
    own = project_keys_values(hidden, *weights[1:])
    far = [lax.ppermute(x, "ctx", ahead) for x in own]
    queries = project_queries(hidden, weights[0])
    far[0], queries = lax.optimization_barrier((far[0], queries))
    d_queries, gradients, waiting = [], [], []

    def finish():
        gown, swapped = waiting.pop()
        total = gown + returned.astype(jnp.float32)
        total = total + jnp.where(odd, 0.0, swapped.astype(jnp.float32))
        gradients.append(total.astype(jnp.bfloat16))

    for h in range(heads):
        near = lax.ppermute(jnp.where(odd, far[h], own[h]), "ctx", swap)
        dq, gfar, gnear, gown = attend(h, queries, cotangent, far[h], near, own[h], low)
        if h > 0:
            gnear, returned = lax.optimization_barrier((gnear, returned))
            finish()
        swapped = lax.ppermute(gnear, "ctx", swap)
        passed = jnp.where(odd, add(gfar, swapped), gfar)
        if h + 1 < heads:
            passed, queries = lax.optimization_barrier((passed, queries))
        returned = lax.ppermute(passed, "ctx", behind)
        d_queries.append(dq)
        waiting.append((gown, swapped))
    finish()

    low_side = plane < 2

    side = jnp.where(low_side, 3, 0)
    step = jnp.where(low_side, -1, 1)
    order = [(side + step * n).astype(jnp.int32) for n in range(planes)]
    last = jnp.where(outer, order[2], order[3])
    home = jnp.where(outer, order[3], order[2])
    grads = (*d_queries, *gradients)
    edge = [
        back_project(order[0].reshape(1), 1, grads, weights, [piece])[0][0] for piece in PIECES
    ]
    sent_outer, sent_middle = [], []

    def send(payload, pairs, sent, depth):
        if len(sent) >= depth:
            payload, _ = lax.optimization_barrier((payload, sent[-depth]))
        sent.append(lax.ppermute(payload, "head", pairs))
        return sent[-1]

    def send_outer(payload, pairs):
        return send(payload, pairs, sent_outer, OUTER_DEPTH)

    def send_middle(payload):
        return send(payload, middle, sent_middle, MIDDLE_DEPTH)

    r0 = [send_outer(block, inward) for block in edge]
    *grads, _ = lax.optimization_barrier((*grads, r0[0]))
    others = jnp.stack([order[1], last, home])
    blocks = back_project(others, 3, grads, weights, PIECES)
    m1 = [send_middle(add(block, r)) for block, r in zip(edge, r0)]
    r1 = [send_outer(block[0], inward) for block in blocks]
    m2 = [send_middle(add(block[0], r)) for block, r in zip(blocks, r1)]
    r2 = [send_outer(add(block[1], m), inward + outward) for block, m in zip(blocks, m1)]
    blocks = [block[2] for block in blocks]
    return jnp.concatenate(
        [
            sum(part.astype(jnp.float32) for part in (block, *parts))
            for block, *parts in zip(blocks, m2, r2)
        ],
        axis=1,
    )


def solution(mesh):
    in_specs = (
        P("ctx", None),
        P(None, "head"),
        P(None, "head"),
        P(None, "head"),
        P("ctx", "head"),
        P("ctx"),
    )
    out_specs = P(("ctx", "head"), None)
    return jax.shard_map(shards, mesh=mesh, in_specs=in_specs, out_specs=out_specs, check_vma=False)
```

```python
import functools

import jax
import jax.numpy as jnp
from jax import lax
from jax.experimental import pallas as pl
from jax.experimental.pallas import tpu as pltpu
from jax.sharding import PartitionSpec as P

HEAD_SIZE = 128
W = 1024
HALO = 2
SCALE = 168.0 ** (-0.5)
LOG2E = 1.4426950408889634
BLOCK = 128
MASKED = -1e30
MIB = 1024 * 1024
KV_CHUNKS = ((0, 768), (768, 1536), (2304, 1536), (3840, 1024), (4864, 512))
Q_CHUNKS = ((0, 768), (768, 1536), (2304, 1536), (3840, 1536))
TILE = 768
PIECES = ((0, 1536), (1536, 1536), (3072, 2304))
OUTER_DEPTH, MIDDLE_DEPTH = 3, 2
PROJECT_LIMIT = 18 * MIB
ATTENTION_LIMIT = 14 * MIB
BACK_LIMIT = 20 * MIB

NT = (((1,), (1,)), ((), ()))


def column_chunks(chunks, hidden_ref, hidden_buf, pairs, sems):
    copies = []
    for at, (first, size) in enumerate(chunks):
        span = pl.ds(first, size)
        group = [pltpu.make_async_copy(hidden_ref.at[:, span], hidden_buf.at[:, span], sems.at[at, 0])]
        for n, (ref, buf) in enumerate(pairs):
            group.append(
                pltpu.make_async_copy(ref.at[span, :], buf.at[span, :], sems.at[at, n + 1])
            )
        for copy in group:
            copy.start()
        copies.append(group)
    return copies


def accumulate(chunks, copies, hidden_buf, bufs):
    totals = [None] * len(bufs)
    for at, (first, size) in enumerate(chunks):
        for copy in copies[at]:
            copy.wait()
        span = slice(first, first + size)
        part = hidden_buf[:, span]
        for n, buf in enumerate(bufs):
            dot = jnp.dot(part, buf[span, :], preferred_element_type=jnp.float32)
            totals[n] = dot if at == 0 else totals[n] + dot
    return totals


def project_kernel(hidden_ref, wk_ref, wv_ref, *refs):
    heads = wk_ref.shape[1] // HEAD_SIZE
    outs, (hidden_buf, k_buf, v_buf, sems) = refs[:heads], refs[heads:]
    copies = column_chunks(
        KV_CHUNKS, hidden_ref, hidden_buf, ((wk_ref, k_buf), (wv_ref, v_buf)), sems
    )
    keys, values = accumulate(KV_CHUNKS, copies, hidden_buf, (k_buf, v_buf))
    for head, out in enumerate(outs):
        cols = slice(head * HEAD_SIZE, (head + 1) * HEAD_SIZE)
        out[:, :HEAD_SIZE] = keys[:, cols].astype(out.dtype)
        out[:, HEAD_SIZE:] = values[:, cols].astype(out.dtype)


def project_keys_values(hidden, wk, wv):
    rows, depth = hidden.shape
    width = wk.shape[1]
    heads = width // HEAD_SIZE
    hbm = pl.BlockSpec(memory_space=pl.ANY)
    vmem = pl.BlockSpec(memory_space=pltpu.VMEM)
    return pl.pallas_call(
        project_kernel,
        in_specs=[hbm] * 3,
        out_specs=[vmem] * heads,
        out_shape=[jax.ShapeDtypeStruct((rows, 2 * HEAD_SIZE), jnp.bfloat16)] * heads,
        scratch_shapes=[
            pltpu.VMEM((rows, depth), jnp.bfloat16),
            pltpu.VMEM((depth, width), jnp.bfloat16),
            pltpu.VMEM((depth, width), jnp.bfloat16),
            pltpu.SemaphoreType.DMA((len(KV_CHUNKS), 3)),
        ],
        compiler_params=pltpu.CompilerParams(vmem_limit_bytes=PROJECT_LIMIT),
        cost_estimate=pl.CostEstimate(
            flops=4 * rows * depth * width,
            bytes_accessed=2 * (rows * depth + 2 * depth * width),
            transcendentals=0,
        ),
        name="project_kv",
    )(hidden, wk, wv)


def query_kernel(hidden_ref, wq_ref, out_ref, hidden_buf, q_buf, sems):
    copies = column_chunks(Q_CHUNKS, hidden_ref, hidden_buf, ((wq_ref, q_buf),), sems)
    (queries,) = accumulate(Q_CHUNKS, copies, hidden_buf, (q_buf,))
    out_ref[...] = queries.astype(out_ref.dtype)


def project_queries(hidden, wq):
    rows, depth = hidden.shape
    width = wq.shape[1]
    hbm = pl.BlockSpec(memory_space=pl.ANY)
    return pl.pallas_call(
        query_kernel,
        in_specs=[hbm] * 2,
        out_specs=pl.BlockSpec(memory_space=pltpu.VMEM),
        out_shape=jax.ShapeDtypeStruct((rows, width), jnp.bfloat16),
        scratch_shapes=[
            pltpu.VMEM((rows, depth), jnp.bfloat16),
            pltpu.VMEM((depth, width), jnp.bfloat16),
            pltpu.SemaphoreType.DMA((len(Q_CHUNKS), 2)),
        ],
        compiler_params=pltpu.CompilerParams(vmem_limit_bytes=PROJECT_LIMIT),
        cost_estimate=pl.CostEstimate(
            flops=2 * rows * depth * width,
            bytes_accessed=2 * (rows * depth + depth * width),
            transcendentals=0,
        ),
        name="project_q",
    )(hidden, wq)


def attention_kernel(
    q_ref, do_ref, far_ref, near_ref, own_ref, low_ref,
    dq_ref, gfar_ref, gnear_ref, gown_ref,
    k_ref, v_ref, dkt_ref, dvt_ref,
):
    rows = q_ref.shape[0]
    window = W + BLOCK
    for at, ref in enumerate((far_ref, near_ref, own_ref)):
        k_ref[at * rows : (at + 1) * rows, :] = ref[:, :HEAD_SIZE]
        v_ref[at * rows : (at + 1) * rows, :] = ref[:, HEAD_SIZE:]
    dkt_ref[...] = jnp.zeros_like(dkt_ref)
    dvt_ref[...] = jnp.zeros_like(dvt_ref)
    for block in range(rows // BLOCK):
        at = slice(block * BLOCK, (block + 1) * BLOCK)
        span = slice(block * BLOCK, block * BLOCK + window)
        q = jnp.concatenate([q_ref[at, :HEAD_SIZE], q_ref[at, HEAD_SIZE:]], axis=0)
        do = jnp.concatenate([do_ref[at, :HEAD_SIZE], do_ref[at, HEAD_SIZE:]], axis=0)
        k = k_ref[span, :]
        v = v_ref[span, :]
        low = low_ref[at, :]
        low = jnp.concatenate([low, low], axis=0) - block * BLOCK
        scores = lax.dot_general(q, k, NT, preferred_element_type=jnp.float32)
        col = lax.broadcasted_iota(jnp.int32, scores.shape, 1)
        row = lax.broadcasted_iota(jnp.int32, scores.shape, 0) & (BLOCK - 1)
        allowed = (col >= low) & (col <= row + W)
        scores = jnp.where(allowed, scores * (SCALE * LOG2E), MASKED)
        top = jnp.max(scores, axis=1, keepdims=True)
        e = jnp.exp2(scores - top)
        inverse = 1.0 / jnp.sum(e, axis=1, keepdims=True)
        probability = e * inverse
        probability_low = probability.astype(jnp.bfloat16)
        d_probs = lax.dot_general(do, v, NT, preferred_element_type=jnp.float32)
        row_dot = jnp.sum(
            probability_low.astype(jnp.float32) * d_probs, axis=1, keepdims=True
        )
        d_scores = (probability * ((d_probs - row_dot) * SCALE)).astype(jnp.bfloat16)
        dq = jnp.dot(d_scores, k, preferred_element_type=jnp.float32).astype(dq_ref.dtype)
        dq_ref[at, :HEAD_SIZE] = dq[:BLOCK]
        dq_ref[at, HEAD_SIZE:] = dq[BLOCK:]
        dkt_ref[:, span] += jnp.dot(q.T, d_scores, preferred_element_type=jnp.float32)
        dvt_ref[:, span] += jnp.dot(do.T, probability_low, preferred_element_type=jnp.float32)
    for at, ref in enumerate((gfar_ref, gnear_ref, gown_ref)):
        part = slice(at * rows, (at + 1) * rows)
        ref[:, :HEAD_SIZE] = dkt_ref[:, part].T.astype(ref.dtype)
        ref[:, HEAD_SIZE:] = dvt_ref[:, part].T.astype(ref.dtype)


def attend(head, queries, cotangent, far, near, own, low):
    rows = queries.shape[0]
    pair = 2 * HEAD_SIZE
    covered = (HALO + 1) * rows
    whole = pl.BlockSpec((rows, pair), lambda i: (0, 0))
    column = pl.BlockSpec((rows, pair), lambda i: (0, head))
    work = 2 * rows * (W + BLOCK) * HEAD_SIZE
    return pl.pallas_call(
        attention_kernel,
        grid=(1,),
        in_specs=[column, column, whole, whole, whole, pl.BlockSpec((rows, 1), lambda i: (0, 0))],
        out_specs=[whole] * 4,
        out_shape=[
            jax.ShapeDtypeStruct((rows, pair), jnp.bfloat16),
            jax.ShapeDtypeStruct((rows, pair), jnp.bfloat16),
            jax.ShapeDtypeStruct((rows, pair), jnp.bfloat16),
            jax.ShapeDtypeStruct((rows, pair), jnp.float32),
        ],
        scratch_shapes=[
            pltpu.VMEM((covered, HEAD_SIZE), jnp.bfloat16),
            pltpu.VMEM((covered, HEAD_SIZE), jnp.bfloat16),
            pltpu.VMEM((HEAD_SIZE, covered), jnp.float32),
            pltpu.VMEM((HEAD_SIZE, covered), jnp.float32),
        ],
        compiler_params=pltpu.CompilerParams(vmem_limit_bytes=ATTENTION_LIMIT),
        cost_estimate=pl.CostEstimate(
            flops=16 * work, bytes_accessed=16 * rows * pair, transcendentals=work // HEAD_SIZE
        ),
        name="attention",
    )(queries, cotangent, far, near, own, low)


def nt(x, w):
    return lax.dot_general(x, w, NT, preferred_element_type=jnp.float32)


def back_kernel(spans, place_ref, dq0_ref, dq1_ref, g0_ref, g1_ref, wq_ref, wk_ref, wv_ref, *refs):
    outs, buf = refs[:-1], refs[-1]
    count = len(outs) // len(spans)
    size = HEAD_SIZE
    pair = 2 * size
    step = pl.program_id(0)

    @pl.when(step == 0)
    def _():
        for n in range(count):
            span = pl.ds(pl.multiple_of(place_ref[n] * size, size), size)
            here = slice(n * size, (n + 1) * size)
            buf[here, :pair] = dq0_ref[span, :]
            buf[here, pair : 2 * pair] = dq1_ref[span, :]
            late = pl.ds(pl.multiple_of(place_ref[count + n] * size, size), size)
            for at, (ref, here_rows) in enumerate(((g0_ref, span), (g1_ref, late))):
                rows = ref[here_rows, :]
                buf[here, 2 * pair + at * size : 2 * pair + (at + 1) * size] = rows[:, :size]
                buf[here, 3 * pair + at * size : 3 * pair + (at + 1) * size] = rows[:, size:]

    total = nt(buf[:, : 2 * pair], wq_ref[...]) + nt(buf[:, 2 * pair : 3 * pair], wk_ref[...])
    total = (total + nt(buf[:, 3 * pair :], wv_ref[...])).astype(jnp.bfloat16)
    for at, (first, steps) in enumerate(spans):

        @pl.when((step >= first) & (step < first + steps))
        def _():
            for n in range(count):
                outs[at * count + n][...] = total[n * size : (n + 1) * size]


def back_project(chunks, count, grads, weights, pieces):
    base = pieces[0][0] // TILE
    spans = [(first // TILE - base, columns // TILE) for first, columns in pieces]
    columns = sum(columns for _, columns in pieces)
    rows = HEAD_SIZE

    def out_spec(first, steps):
        return pl.BlockSpec((rows, TILE), lambda j, place: (0, jnp.clip(j - first, 0, steps - 1)))

    grid_spec = pltpu.PrefetchScalarGridSpec(
        num_scalar_prefetch=1,
        grid=(columns // TILE,),
        in_specs=[pl.BlockSpec(x.shape, lambda j, place: (0, 0)) for x in grads]
        + [pl.BlockSpec((TILE, w.shape[1]), lambda j, place: (base + j, 0)) for w in weights],
        out_specs=[out_spec(*span) for span in spans for _ in range(count)],
        scratch_shapes=[pltpu.VMEM((count * rows, 1024), jnp.bfloat16)],
    )
    outs = pl.pallas_call(
        functools.partial(back_kernel, spans),
        grid_spec=grid_spec,
        out_shape=[
            jax.ShapeDtypeStruct((rows, columns), jnp.bfloat16)
            for _, columns in pieces
            for _ in range(count)
        ],
        compiler_params=pltpu.CompilerParams(vmem_limit_bytes=BACK_LIMIT),
        cost_estimate=pl.CostEstimate(
            flops=2 * count * rows * columns * 1024,
            bytes_accessed=2 * columns * (1024 + count * rows),
            transcendentals=0,
        ),
        name="back_project",
    )(chunks, *grads, *weights)
    return [outs[at * count : (at + 1) * count] for at in range(len(pieces))]


def add(a, b):
    return (a.astype(jnp.float32) + b.astype(jnp.float32)).astype(jnp.bfloat16)


def shards(hidden, w_query, w_key, w_value, cotangent, doc_start):
    rows = hidden.shape[0]
    contexts = lax.axis_size("ctx")
    planes = lax.axis_size("head")
    ctx = lax.axis_index("ctx")
    plane = lax.axis_index("head")
    odd = (ctx % 2) == 1
    outer = (plane == 0) | (plane == planes - 1)
    heads = w_key.shape[1] // HEAD_SIZE
    chunk = rows // planes
    swap = [(i, i ^ 1) for i in range(contexts)]
    ahead = [(i, i + 2) for i in range(contexts - 2)]
    behind = [(i + 2, i) for i in range(contexts - 2)]
    inward = [(0, 1), (3, 2)]
    middle = [(1, 2), (2, 1)]
    outward = [(1, 0), (2, 3)]
    hidden, *weights = (
        pltpu.with_memory_space_constraint(x, pltpu.HBM)
        for x in (hidden, w_query, w_key, w_value)
    )

    low = jnp.maximum(
        doc_start - ctx * rows + HALO * rows,
        jnp.arange(rows, dtype=jnp.int32) + (HALO * rows - W + 1),
    ).reshape(rows, 1)
    own = project_keys_values(hidden, *weights[1:])
    far = [lax.ppermute(x, "ctx", ahead) for x in own]
    queries = project_queries(hidden, weights[0])
    far[0], queries = lax.optimization_barrier((far[0], queries))
    d_queries, gradients, waiting = [], [], []

    def finish():
        gown, swapped = waiting.pop()
        total = gown + returned.astype(jnp.float32)
        total = total + jnp.where(odd, 0.0, swapped.astype(jnp.float32))
        gradients.append(total.astype(jnp.bfloat16))

    for h in range(heads):
        near = lax.ppermute(jnp.where(odd, far[h], own[h]), "ctx", swap)
        dq, gfar, gnear, gown = attend(h, queries, cotangent, far[h], near, own[h], low)
        if h > 0:
            gnear, returned = lax.optimization_barrier((gnear, returned))
            finish()
        swapped = lax.ppermute(gnear, "ctx", swap)
        passed = jnp.where(odd, add(gfar, swapped), gfar)
        if h + 1 < heads:
            passed, queries = lax.optimization_barrier((passed, queries))
        d_queries.append(dq)
        waiting.append((gown, swapped))
        if h + 1 < heads:
            returned = lax.ppermute(passed, "ctx", behind)

    low_side = plane < 2
    gown, swapped = waiting.pop()
    local = gown + jnp.where(odd, 0.0, swapped.astype(jnp.float32))

    def come_back(first, count, *after):
        part = lax.dynamic_slice_in_dim(passed, first, count, 0)
        if after:
            part, *_ = lax.optimization_barrier((part, *after))
        part = lax.ppermute(part, "ctx", behind).astype(jnp.float32)
        part = lax.dynamic_slice_in_dim(local, first, count, 0) + part
        return part.astype(jnp.bfloat16)

    early = come_back(jnp.where(low_side, rows - chunk, 0), chunk)

    side = jnp.where(low_side, 3, 0)
    step = jnp.where(low_side, -1, 1)
    order = [(side + step * n).astype(jnp.int32) for n in range(planes)]
    last = jnp.where(outer, order[2], order[3])
    home = jnp.where(outer, order[3], order[2])
    grads = (*d_queries, *gradients, early)
    zero = jnp.zeros((), jnp.int32)
    edge = [
        back_project(jnp.stack([order[0], zero]), 1, grads, weights, [piece])[0][0]
        for piece in PIECES
    ]
    sent_outer, sent_middle = [], []

    def send(payload, pairs, sent, depth):
        if len(sent) >= depth:
            payload, _ = lax.optimization_barrier((payload, sent[-depth]))
        sent.append(lax.ppermute(payload, "head", pairs))
        return sent[-1]

    def send_outer(payload, pairs):
        return send(payload, pairs, sent_outer, OUTER_DEPTH)

    def send_middle(payload):
        return send(payload, middle, sent_middle, MIDDLE_DEPTH)

    r0 = [send_outer(block, inward) for block in edge]
    late_rows = come_back(jnp.where(low_side, 0, chunk), rows - chunk, r0[0])
    *grads, _ = lax.optimization_barrier((*grads[:-1], late_rows, r0[0]))
    others = [order[1], last, home]
    late = jnp.where(low_side, 0, 1).astype(jnp.int32)
    others = jnp.stack(others + [at - late for at in others])
    blocks = back_project(others, 3, grads, weights, PIECES[:1])
    blocks += back_project(others, 3, grads, weights, PIECES[1:])
    m1 = [send_middle(add(block, r)) for block, r in zip(edge, r0)]
    r1 = [send_outer(block[0], inward) for block in blocks]
    m2 = [send_middle(add(block[0], r)) for block, r in zip(blocks, r1)]
    r2 = [send_outer(add(block[1], m), inward + outward) for block, m in zip(blocks, m1)]
    blocks = [block[2] for block in blocks]
    return jnp.concatenate(
        [
            sum(part.astype(jnp.float32) for part in (block, *parts))
            for block, *parts in zip(blocks, m2, r2)
        ],
        axis=1,
    )


def solution(mesh):
    in_specs = (
        P("ctx", None),
        P(None, "head"),
        P(None, "head"),
        P(None, "head"),
        P("ctx", "head"),
        P("ctx"),
    )
    out_specs = P(("ctx", "head"), None)
    return jax.shard_map(shards, mesh=mesh, in_specs=in_specs, out_specs=out_specs, check_vma=False)
```
